256 devices in a mesh: group: 8 (over y, core), slab: 32 (over x, z).
Axes of the slice: x: 4, y: 4, z: 8, core: 2. Of those that a mesh axis runs over, the one named last changes fastest.
Arguments:
- volume: bfloat16 [32768, 2, 384], P('slab'), may hold values from -6 to 6
- weight_tiles: bfloat16 [4, 384, 384], replicated, may hold values from 0 to 0.08984375
- ctf_table: float32 [8, 48, 384], replicated, may hold values from -1 to 1
- observed: bfloat16 [2048, 48, 2, 384], P(('group', 'slab')), may hold values from -6 to 6
- routes: int32 [2048, 48, 2], P(('group', 'slab')), may hold values from 0 to 127, all different within a row; in each aligned block of 384 rows (0 to 383, 384 to 767, ..., all dimensions but the last counted through in order) at most 12 rows name the same one
- piece_index: int32 [2048, 48, 2], P(('group', 'slab')), may hold values from 0 to 1023
- pose_index: int32 [2048], P(('group', 'slab')), may hold values from 0 to 31
- ctf_class: int32 [2048], P(('group', 'slab')), may hold values from 0 to 7
Outputs:
- back_projected: float32 [32768, 2, 384], P('slab')
- residuals: bfloat16 [2048, 48, 2, 384], P(('group', 'slab'))
The draws below stay inside these ranges and needn't reach their ends.
Inputs may be any that keep to these rules, and one draw needn't show every extreme that they name: routes // 4 is the slab device holding the reference line, routes % 4 the tile; the two entries of a line differ; the lines of one device name each value at most 12 times, a bound that some block reaches.
All inputs are finite; a program needn't handle non-finite values.
Results may differ from the reference program's by a relative error of at most 0.012.
Values may be sent and summed in bfloat16 or wider, within the bound.
A program may use at most 64 MiB of HBM per device.

```python
import math
import jax
import jax.numpy as jnp
import numpy as np
from jax import lax

BOX = 384
TILES = 4
CTF_CLASSES = 8
POSES = 32
IMG_DEV = 8
LINES = 48
PIECES_DEV = 1024
BUCKETS = 128
CAP = 12
IMAGES = 2048
PIECES = 32768
N_GROUP = 8
N_SLAB = 32


def plant(drawn, rng, least, largest):
    dims = drawn.shape
    place = [jax.random.randint(jax.random.fold_in(rng, axis), (), 0, dims[axis]) for axis in range(len(dims))]
    drawn = drawn.at[tuple(place)].set(least)
    longest = dims.index(max(dims))
    place[longest] = (place[longest] + 1) % dims[longest]
    return drawn.at[tuple(place)].set(largest)


def block_scale(own_key, dims, cuts, smallest, top_value):
    level, own = 1.0, jax.random.fold_in(own_key, 6)
    for position, parts in cuts:
        heights = jnp.exp(jax.random.uniform(jax.random.fold_in(own, position), (parts,), jnp.float32, smallest / len(cuts), top_value / len(cuts)))
        level = level * jnp.repeat(heights, dims[position] // parts).reshape([-1 if axis == position else 1 for axis in range(len(dims))])
    return level


def shared_out(stream_key, own, number, rows, number_of, top, most, slope):
    ranking = jax.random.permutation(stream_key, number_of)
    heavy_load, usual = load_shares(number_of, rows * top, most, slope, True), load_shares(number_of, rows * top, most, slope, False)
    places = jnp.arange(number_of)

    def named(sizes, turn):
        used = int((sizes > 0).sum())
        fixed = max(1, used // 4)
        shifted = fixed + (places - fixed + turn * (used - fixed)) % max(1, number_of - fixed)
        return jnp.zeros((number_of,), jnp.int32).at[ranking[jnp.where(places < fixed, places, shifted)]].set(jnp.asarray(sizes, jnp.int32))

    sizes = jnp.where(number % 4 == 0, named(heavy_load, number // 4), named(usual, number - number // 4 - 1))
    mixed = jax.random.permutation(jax.random.fold_in(own, 3), number_of)
    giver, taker = mixed[0:number_of // 2 * 2:2], mixed[1:number_of // 2 * 2:2]
    slack = jnp.minimum(sizes[giver] - 1, most - sizes[taker]) // 2
    slack = jnp.where((giver == ranking[0]) | (taker == ranking[0]) | (sizes[taker] == 0), 0, jnp.maximum(slack, 0))
    shifted = jax.random.randint(jax.random.fold_in(own, 4), (number_of // 2,), 0, 1 << 20) % (slack + 1)
    sizes = sizes.at[giver].add(-shifted).at[taker].add(shifted)
    items = jnp.searchsorted(jnp.cumsum(sizes), jnp.arange(rows * top), side="right").astype(jnp.int32)
    grid = items.reshape(top, rows).T
    grid = grid[jax.random.permutation(jax.random.fold_in(own, 1), rows)]
    turn = jax.random.randint(jax.random.fold_in(own, 2), (rows, 1), 0, top)
    return jnp.take_along_axis(grid, (jnp.arange(top)[None, :] + turn) % top, axis=1)


def load_shares(amount, total, limit, slope, full):
    portions = [(1 << 20) // math.isqrt(grade ** slope) + 1 for grade in range(1, amount + 1)]
    largest = limit if full else min(limit, max(-(-total // amount), total * portions[0] // sum(portions)))
    least = 1 if total - largest >= amount - 1 else 0
    given, rest = [largest] + [least] * (amount - 1), total - largest - least * (amount - 1)
    while rest > 0:
        candidates = [i for i in range(1, amount) if given[i] < largest] or [i for i in range(1, amount) if given[i] < limit]
        whole, remaining = sum([portions[i] for i in candidates]), rest
        for i in candidates:
            extra = min(limit - given[i], max(1, remaining * portions[i] // whole), rest)
            given[i] = given[i] + extra
            rest = rest - extra
    return np.array(given)


def noise(key, dims, deviation, reach, pieces=(), held_as=jnp.bfloat16):
    result = jax.random.normal(key, dims, jnp.float32) * deviation
    if len(pieces) > 0:
        result = block_scale(key, dims, pieces, -0.22, 0.18) * result
    return jnp.clip(result, min=-reach, max=reach).astype(held_as)


def setup_inputs(seed: int = 0) -> dict:
    key_list = jax.random.split(jax.random.key(seed), 9)
    volume = noise(key_list[0], (PIECES, 2, BOX), 1.0, 6.0, ((0, 32),))
    weight_tiles = jnp.clip(jax.random.uniform(key_list[1], (TILES, BOX, BOX), jnp.float32, 0.0, 0.08984375), 0.0, 0.08984375).astype(jnp.bfloat16)
    ctf_table = jnp.clip(jax.random.uniform(key_list[2], (CTF_CLASSES, LINES, BOX), jnp.float32, -1.0, 1.0), -1.0, 1.0)
    observed = noise(key_list[3], (IMAGES, LINES, 2, BOX), 1.0, 6.0, ((0, 256),))
    routes_keys = jax.random.split(jax.random.fold_in(key_list[4], 1), IMAGES * LINES // (IMG_DEV * LINES))
    routes_turns = jax.random.permutation(jax.random.fold_in(key_list[4], 3), IMAGES * LINES // (IMG_DEV * LINES))
    routes = jax.vmap(lambda own, number: shared_out(jax.random.fold_in(key_list[4], 2), own, number, IMG_DEV * LINES, BUCKETS, 2, CAP, 2))(routes_keys, routes_turns).reshape((IMAGES, LINES, 2))
    piece_index = plant(jax.random.randint(key_list[5], (IMAGES, LINES, 2), 0, PIECES_DEV), jax.random.fold_in(key_list[5], 1), 0, PIECES_DEV - 1).astype(jnp.int32)
    pose_index = plant(jax.random.randint(key_list[6], (IMAGES,), 0, POSES), jax.random.fold_in(key_list[6], 1), 0, POSES - 1).astype(jnp.int32)
    ctf_class = plant(jax.random.randint(key_list[7], (IMAGES,), 0, CTF_CLASSES), jax.random.fold_in(key_list[7], 1), 0, CTF_CLASSES - 1).astype(jnp.int32)
    return {"volume": volume, "weight_tiles": weight_tiles, "ctf_table": ctf_table, "observed": observed, "routes": routes, "piece_index": piece_index, "pose_index": pose_index, "ctf_class": ctf_class}


def reference(volume, weight_tiles, ctf_table, observed, routes, piece_index, pose_index, ctf_class):
    piece_count = volume.shape[0]
    flat_volume = volume.reshape(piece_count * 2, BOX)
    proj_table = jnp.stack([jnp.dot(flat_volume, weight_tiles[tile_num], preferred_element_type=jnp.float32).reshape(piece_count, 2, BOX) for tile_num in range(TILES)]).astype(jnp.bfloat16)
    wavenumber = jnp.arange(BOX).astype(jnp.float32)
    group_images = IMG_DEV * N_SLAB

    def one_group(totals, inputs):
        obs_block, route_block, piece_block, pose_block, class_block = inputs
        tile_of = route_block % TILES
        global_piece = (route_block // TILES) * PIECES_DEV + piece_block
        contrib = proj_table[tile_of, global_piece]
        projected = contrib[:, :, 0].astype(jnp.float32) + contrib[:, :, 1].astype(jnp.float32)
        shifts = (pose_block - POSES // 2).astype(jnp.float32)
        phases = 2.0 * jnp.pi * shifts[:, None] * wavenumber[None, :] / BOX
        cos_table = jnp.cos(phases)[:, None, :]
        sin_table = jnp.sin(phases)[:, None, :]
        real_part = projected[:, :, 0] * cos_table - projected[:, :, 1] * sin_table
        imag_part = projected[:, :, 0] * sin_table + projected[:, :, 1] * cos_table
        ctf_lines = ctf_table[class_block]
        res_real = obs_block[:, :, 0].astype(jnp.float32) - ctf_lines * real_part
        res_imag = obs_block[:, :, 1].astype(jnp.float32) - ctf_lines * imag_part
        residual = jnp.stack([res_real, res_imag], axis=2).astype(jnp.bfloat16)
        weighted_real = ctf_lines * res_real
        weighted_imag = ctf_lines * res_imag
        back_real = weighted_real * cos_table + weighted_imag * sin_table
        back_imag = weighted_imag * cos_table - weighted_real * sin_table
        returned = jnp.stack([back_real, back_imag], axis=2).astype(jnp.bfloat16)
        returned = lax.optimization_barrier(returned).astype(jnp.float32)
        slot_rows = jnp.broadcast_to(returned[:, :, None], contrib.shape).reshape(-1, 2, BOX)
        segments = (tile_of * piece_count + global_piece).reshape(-1).astype(jnp.int32)
        totals = totals + jax.ops.segment_sum(slot_rows, segments, num_segments=TILES * piece_count)
        return totals, residual

    inputs = (observed.reshape(N_GROUP, group_images, LINES, 2, BOX),
              routes.reshape(N_GROUP, group_images, LINES, 2),
              piece_index.reshape(N_GROUP, group_images, LINES, 2),
              pose_index.reshape(N_GROUP, group_images),
              ctf_class.reshape(N_GROUP, group_images))
    start = jnp.zeros((TILES * piece_count, 2, BOX), jnp.float32)
    totals, residuals = lax.scan(one_group, start, inputs)
    totals = totals.reshape(TILES, piece_count * 2, BOX)
    back_projected = jnp.zeros((piece_count * 2, BOX), jnp.float32)
    for tile_num in range(TILES):
        back_projected = back_projected + jnp.dot(totals[tile_num], weight_tiles[tile_num].astype(jnp.float32).T, precision=lax.Precision.HIGHEST)
    return back_projected.reshape(piece_count, 2, BOX), residuals.reshape(-1, LINES, 2, BOX)
```

```python
import functools

import jax
import jax.numpy as jnp
from jax import lax
from jax.experimental import pallas as pl
from jax.experimental.pallas import tpu as pltpu
from jax.sharding import PartitionSpec as P

MESH = pl.DeviceIdType.MESH
POSES = 32
CORES = 2
BATCHES = 4
BF = jnp.bfloat16
F32 = jnp.float32
NT = (((1,), (1,)), ((), ()))


def mm(a, b):
    return jnp.dot(a, b, preferred_element_type=F32)


def iota(shape, axis):
    return lax.broadcasted_iota(jnp.int32, shape, axis)


def kernel(
    cfg,
    pose_ref, cls_ref, req_ref, vol_ref, w_ref, ctf_ref, obs_ref,
    back_ref, res_ref,
    code_out, code_in, code_rows, hot, send1, recv1, pick, place, proj, ret, send2, recv2, rows_back, total,
    core_out, core_in, y_out, y_in, result,
    code_ss, code_rs, ss1, rs1, ss2, rs2, core_ss, core_rs, y_ss, y_rs, ag_ss, ag_rs, sib_ss, sib_rs,
):
    nx, nz, ny, tiles, cap, lines = cfg
    slabs = nx * nz
    groups = ny * CORES
    per = slabs // BATCHES
    chunk = tiles * cap
    rows = per * chunk
    items = req_ref.shape[1]
    pieces, width = vol_ref.shape
    box = width // 2
    shard = pieces // groups
    images = items // lines

    slab, group = lax.axis_index("slab"), lax.axis_index("group")
    my_x, my_z = slab // nz, slab % nz
    my_y, core = group // CORES, group % CORES
    sibling = {"group": my_y * CORES + 1 - core}

    def partner(k, sign):
        step = k % nz
        dz = (step % 2) * ((step + 1) // 2) + (1 - step % 2) * (nz - step // 2)
        dx = k // nz
        x = (my_x + nx + sign * dx) % nx
        z = (my_z + 2 * nz + sign * dz) % nz
        return {"slab": x * nz + z}

    def y_peer(dy):
        return {"group": (my_y + dy) % ny * CORES + core}

    barrier = pltpu.get_barrier_semaphore()

    def greet(k, carry):
        pl.semaphore_signal(barrier, inc=1, device_id=partner(k, 1), device_id_type=MESH)
        return carry

    lax.fori_loop(1, slabs, greet, 0)
    pl.semaphore_signal(barrier, inc=1, device_id=sibling, device_id_type=MESH)
    for dy in range(1, ny):
        pl.semaphore_signal(barrier, inc=1, device_id=y_peer(dy), device_id_type=MESH)

    req = req_ref[...]
    req = jnp.concatenate([req[0:1], req[1:2]], axis=1)
    bucket, piece = req >> 10, req & 1023
    tile, owner = bucket % tiles, bucket // tiles
    dx = (owner // nz + nx - my_x) % nx
    dz = (owner % nz + nz - my_z) % nz
    step = jnp.maximum(jnp.where(dz <= nz // 2, 2 * dz - 1, 2 * (nz - dz)), 0)
    server = dx * nz + step
    both = 2 * items
    own = iota((slabs * tiles, both), 0) == server * tiles + tile
    before = (iota((both, both), 0) < iota((both, both), 1)).astype(F32).astype(BF)
    earlier = mm(own.astype(F32).astype(BF), before)
    rank = jnp.sum(jnp.where(own, earlier, 0.0), axis=0, keepdims=True).astype(jnp.int32)
    seat = tile * cap + rank
    spot = server * chunk + seat
    to_server = (iota((slabs, both), 0) == server).astype(F32).astype(BF)
    at_seat = iota((128, both), 0) == seat
    low = jnp.where(at_seat, (piece & 31).astype(F32), 0.0).astype(BF)
    high = jnp.where(at_seat, (piece >> 5).astype(F32), 0.0).astype(BF)
    codes = lax.dot_general(to_server, low, NT, preferred_element_type=F32)
    codes = codes + 32.0 * lax.dot_general(to_server, high, NT, preferred_element_type=F32)
    codes = codes.astype(jnp.int32)
    for k in range(slabs):
        code_out[k] = codes[k : k + 1]
    code_in[0] = codes[0:1]

    def code_copy(k):
        return pltpu.make_async_remote_copy(
            src_ref=code_out.at[k], dst_ref=code_in.at[k], send_sem=code_ss.at[k], recv_sem=code_rs.at[k],
            device_id=partner(k, 1), device_id_type=MESH,
        )

    def answer_copy(k):
        return pltpu.make_async_remote_copy(
            src_ref=send1.at[k], dst_ref=recv1.at[k], send_sem=ss1.at[k], recv_sem=rs1.at[k],
            device_id=partner(k, -1), device_id_type=MESH,
        )

    def return_copy(k):
        return pltpu.make_async_remote_copy(
            src_ref=send2.at[k], dst_ref=recv2.at[k], send_sem=ss2.at[k], recv_sem=rs2.at[k],
            device_id=partner(k, 1), device_id_type=MESH,
        )

    def each(first, last, action):
        def body(k, carry):
            action(k)
            return carry

        lax.fori_loop(first, last, body, 0)

    pl.semaphore_wait(barrier, slabs - 1 + ny)
    each(1, slabs, lambda k: code_copy(k).start())

    spot0, spot1 = spot[:, :items], spot[:, items:]
    diagonal = iota((items, items), 0) == iota((items, items), 1)
    col0 = jnp.sum(jnp.where(diagonal, spot0.astype(F32), 0.0), axis=1, keepdims=True).astype(jnp.int32)
    col1 = jnp.sum(jnp.where(diagonal, spot1.astype(F32), 0.0), axis=1, keepdims=True).astype(jnp.int32)
    for b in range(BATCHES):
        across = iota((items, rows), 1) + b * rows
        pick[b] = ((across == col0) | (across == col1)).astype(F32).astype(BF)
        down = iota((rows, items), 0) + b * rows
        place[b] = ((down == spot0) | (down == spot1)).astype(F32).astype(BF)

    row_tile = iota((rows, box), 0) % chunk // cap

    def serve(b, carry):
        for c in range(per):
            k = b * per + c

            @pl.when(k > 0)
            def _():
                code_copy(k).wait_recv()

        line = jnp.zeros((1, rows), F32)
        for c in range(per):
            code = code_in[b * per + c].astype(F32)
            eye = iota((chunk, 128), 0) == iota((chunk, 128), 1)
            col = jnp.sum(jnp.where(eye, code, 0.0), axis=1, keepdims=True)
            spread = iota((chunk, rows), 0) + c * chunk == iota((chunk, rows), 1)
            line = line + jnp.sum(jnp.where(spread, col, 0.0), axis=0, keepdims=True)
            hot[c * chunk : (c + 1) * chunk] = (iota((chunk, pieces), 1) == col.astype(jnp.int32)).astype(F32).astype(BF)
        code_rows[b] = line.astype(jnp.int32)
        fetched = mm(hot[...], vol_ref[...])
        for part in range(2):
            half = fetched[:, part * box : (part + 1) * box]
            answer = jnp.zeros((rows, box), F32)
            for t in range(tiles):
                answer = answer + mm(jnp.where(row_tile == t, half, 0.0).astype(BF), w_ref[t])
            send1[pl.ds(b * per, per), :, part * box : (part + 1) * box] = answer.astype(BF).reshape(per, chunk, box)
        for c in range(per):
            k = b * per + c

            @pl.when(k > 0)
            def _():
                answer_copy(k).start()

        return carry

    lax.fori_loop(0, BATCHES, serve, 0)
    recv1[0] = send1[0]

    number = iota((images, box), 0)
    shift = jnp.zeros((images, box), F32)
    for i in range(images):
        shift = jnp.where(number == i, (pose_ref[i] - POSES // 2).astype(F32), shift)
    phases = 2.0 * jnp.pi * shift * iota((images, box), 1).astype(F32) / box
    cos_table, sin_table = jnp.cos(phases), jnp.sin(phases)

    proj[...] = jnp.zeros_like(proj)

    def collect(b, carry):
        for c in range(per):
            k = b * per + c

            @pl.when(k > 0)
            def _():
                answer_copy(k).wait_recv()

        proj[...] += mm(pick[b], recv1[pl.ds(b * per, per)].reshape(rows, width))
        return carry

    lax.fori_loop(0, BATCHES, collect, 0)

    for i in range(images):
        at = slice(i * lines, (i + 1) * lines)
        real, imag = proj[at, :box], proj[at, box:]
        cos, sin = cos_table[i : i + 1], sin_table[i : i + 1]
        ctf = ctf_ref[cls_ref[i]]
        res_real = obs_ref[at, :box].astype(F32) - ctf * (real * cos - imag * sin)
        res_imag = obs_ref[at, box:].astype(F32) - ctf * (real * sin + imag * cos)
        res_ref[at, :box] = res_real.astype(BF)
        res_ref[at, box:] = res_imag.astype(BF)
        real, imag = ctf * res_real, ctf * res_imag
        ret[at, :box] = (real * cos + imag * sin).astype(BF)
        ret[at, box:] = (imag * cos - real * sin).astype(BF)

    def give_back(b, carry):
        filled = mm(place[b], ret[...]).astype(BF)
        send2[pl.ds(b * per, per)] = filled.reshape(per, chunk, width)
        for c in range(per):
            k = b * per + c

            @pl.when(k > 0)
            def _():
                return_copy(k).start()

        return carry

    lax.fori_loop(0, BATCHES, give_back, 0)
    recv2[0] = send2[0]
    total[...] = jnp.zeros_like(total)

    def add_shard(b, m):
        at_piece = iota((shard, rows), 0) + m * shard == code_rows[b]
        total[m] += mm(at_piece.astype(F32).astype(BF), rows_back[...])

    def absorb(b, carry):
        for c in range(per):
            k = b * per + c

            @pl.when(k > 0)
            def _():
                return_copy(k).wait_recv()

        got = recv2[pl.ds(b * per, per)].reshape(rows, width).astype(F32)
        for part in range(2):
            half = got[:, part * box : (part + 1) * box]
            back = jnp.zeros((rows, box), F32)
            for t in range(tiles):
                masked = jnp.where(row_tile == t, half, 0.0).astype(BF)
                back = back + lax.dot_general(masked, w_ref[t], NT, preferred_element_type=F32)
            rows_back[:, part * box : (part + 1) * box] = back.astype(BF)

        @pl.when(b < BATCHES - 1)
        def _():
            each(0, groups, lambda m: add_shard(b, m))

        return carry

    lax.fori_loop(0, BATCHES, absorb, 0)

    def core_copy(d):
        return pltpu.make_async_remote_copy(
            src_ref=core_out.at[d], dst_ref=core_in.at[d], send_sem=core_ss.at[d], recv_sem=core_rs.at[d],
            device_id=sibling, device_id_type=MESH,
        )

    def y_copy(d):
        return pltpu.make_async_remote_copy(
            src_ref=y_out.at[d], dst_ref=y_in.at[d], send_sem=y_ss.at[d], recv_sem=y_rs.at[d],
            device_id=y_peer(d), device_id_type=MESH,
        )

    def spread_copy(d):
        return pltpu.make_async_remote_copy(
            src_ref=result.at[group], dst_ref=result.at[group], send_sem=ag_ss.at[d], recv_sem=ag_rs.at[d],
            device_id=y_peer(d), device_id_type=MESH,
        )

    def sibling_copy(d):
        m = (my_y + ny - d) % ny * CORES + core
        return pltpu.make_async_remote_copy(
            src_ref=result.at[m], dst_ref=result.at[m], send_sem=sib_ss.at[d], recv_sem=sib_rs.at[d],
            device_id=sibling, device_id_type=MESH,
        )

    order = [*range(1, ny), 0]
    last = BATCHES - 1
    for d in order:
        m = (my_y + d) % ny * CORES + 1 - core
        add_shard(last, m)
        core_out[d] = total[m].astype(BF)
        core_copy(d).start()
    for d in order:
        add_shard(last, (my_y + d) % ny * CORES + core)
    for d in order:
        m = (my_y + d) % ny * CORES + core
        core_copy(d).wait_recv()
        total[m] += core_in[d].astype(F32)
        if d > 0:
            y_out[d] = total[m].astype(BF)
            y_copy(d).start()
    for d in range(1, ny):
        y_copy(d).wait_recv()
        total[group] += y_in[d].astype(F32)
    result[group] = total[group].astype(BF)
    for d in range(1, ny):
        spread_copy(d).start()
    sibling_copy(0).start()
    for d in range(1, ny):
        spread_copy(d).wait_recv()
        sibling_copy(d).start()
    for d in range(ny):
        sibling_copy(d).wait_recv()
    back_ref[...] = result[...].reshape(pieces, width)

    def drain(k):
        code_copy(k).wait_send()
        answer_copy(k).wait_send()
        return_copy(k).wait_send()

    each(1, slabs, drain)
    for d in range(ny):
        core_copy(d).wait_send()
        sibling_copy(d).wait_send()
        if d > 0:
            y_copy(d).wait_send()
            spread_copy(d).wait_send()


def on_device(nx, nz, ny, volume, weight_tiles, ctf_table, observed, routes, piece_index, pose_index, ctf_class):
    pieces, _, box = volume.shape
    images, lines = observed.shape[:2]
    items = images * lines
    tiles = weight_tiles.shape[0]
    slabs, groups = nx * nz, ny * CORES
    cap = max(2, 4 * items // (slabs * tiles))
    per = slabs // BATCHES
    chunk = tiles * cap
    rows = per * chunk
    width = 2 * box
    shard = pieces // groups
    requests = (routes * 1024 + piece_index).transpose(2, 0, 1).reshape(2, items)
    vmem, smem = pl.BlockSpec(memory_space=pltpu.VMEM), pl.BlockSpec(memory_space=pltpu.SMEM)
    dma = pltpu.SemaphoreType.DMA
    back, residual = pl.pallas_call(
        functools.partial(kernel, (nx, nz, ny, tiles, cap, lines)),
        out_shape=(jax.ShapeDtypeStruct((pieces, width), BF), jax.ShapeDtypeStruct((items, width), BF)),
        in_specs=[smem, smem, vmem, vmem, vmem, vmem, vmem],
        out_specs=(vmem, vmem),
        scratch_shapes=[
            pltpu.VMEM((slabs, 1, 128), jnp.int32),
            pltpu.VMEM((slabs, 1, 128), jnp.int32),
            pltpu.VMEM((BATCHES, 1, rows), jnp.int32),
            pltpu.VMEM((rows, pieces), BF),
            pltpu.VMEM((slabs, chunk, width), BF),
            pltpu.VMEM((slabs, chunk, width), BF),
            pltpu.VMEM((BATCHES, items, rows), BF),
            pltpu.VMEM((BATCHES, rows, items), BF),
            pltpu.VMEM((items, width), F32),
            pltpu.VMEM((items, width), BF),
            pltpu.VMEM((slabs, chunk, width), BF),
            pltpu.VMEM((slabs, chunk, width), BF),
            pltpu.VMEM((rows, width), BF),
            pltpu.VMEM((groups, shard, width), F32),
            pltpu.VMEM((ny, shard, width), BF),
            pltpu.VMEM((ny, shard, width), BF),
            pltpu.VMEM((ny, shard, width), BF),
            pltpu.VMEM((ny, shard, width), BF),
            pltpu.VMEM((groups, shard, width), BF),
            *[dma((slabs,))] * 6,
            *[dma((ny,))] * 8,
        ],
        compiler_params=pltpu.CompilerParams(collective_id=0, has_side_effects=True, vmem_limit_bytes=56 * 2**20),
    )(
        pose_index, ctf_class, requests, volume.reshape(pieces, width), weight_tiles, ctf_table,
        observed.reshape(items, width),
    )
    return back.reshape(pieces, 2, box).astype(F32), residual.reshape(images, lines, 2, box)


def solution(mesh):
    slabs, groups = mesh.shape["slab"], mesh.shape["group"]
    nz = 8 if slabs % 8 == 0 else 2
    by_device = ("group", "slab")
    return jax.shard_map(
        functools.partial(on_device, slabs // nz, nz, groups // CORES),
        mesh=mesh,
        in_specs=(
            P("slab", None, None), P(), P(), P(by_device, None, None, None), P(by_device, None, None),
            P(by_device, None, None), P(by_device), P(by_device),
        ),
        out_specs=(P("slab", None, None), P(by_device, None, None, None)),
        check_vma=False,
    )
```

```python
import functools

import jax
import jax.numpy as jnp
from jax import lax
from jax.experimental import pallas as pl
from jax.experimental.pallas import tpu as pltpu
from jax.sharding import PartitionSpec as P

MESH = pl.DeviceIdType.MESH
POSES = 32
CORES = 2
BATCHES = 4
PARTS = 4
STEPS = 8
TOGETHER = 2
BF = jnp.bfloat16
F32 = jnp.float32
NT = (((1,), (1,)), ((), ()))


def mm(a, b):
    return jnp.dot(a, b, preferred_element_type=F32)


def iota(shape, axis):
    return lax.broadcasted_iota(jnp.int32, shape, axis)


def kernel(
    cfg,
    pose_ref, cls_ref, req_ref, vol_ref, w_ref, ctf_ref, obs_ref,
    back_ref, res_ref,
    held, code_out, code_in, sum_out, sum_in, code_rows, hot, send1, recv1, pick, place, proj, ret, send2, recv2, rows_back, total,
    chain_out, chain_in, root_in, result,
    half_ss, half_rs, share_ss, share_rs, code_ss, code_rs, sum_ss, sum_rs, ss1, rs1, ss2, rs2, chain_ss, chain_rs, root_rs, up_ss, down_ss, y_rs, sib_ss, sib_rs,
):
    nx, nz, ny, tiles, cap, lines = cfg
    slabs = nx * nz
    per = slabs // BATCHES
    chunk = tiles * cap
    rows = per * chunk
    items = req_ref.shape[1]
    part_rows, width = vol_ref.shape[1:]
    pieces = ny * PARTS * part_rows
    box = width // 2
    sum_rows = pieces // STEPS
    rows_added = TOGETHER * sum_rows
    images = items // lines

    slab, group = lax.axis_index("slab"), lax.axis_index("group")
    my_x, my_z = slab // nz, slab % nz
    my_y, core = group // CORES, group % CORES
    sibling = {"group": my_y * CORES + 1 - core}

    near = nz // 4

    def at(x, z, c):
        return {"slab": (my_x + nx + x) % nx * nz + (my_z + 2 * nz + z) % nz, "group": my_y * CORES + (core + c) % CORES}

    def two_ways(j):
        return j % 2 * ((j + 1) // 2) - (1 - j % 2) * (j // 2)

    def server(k, sign):
        j = k % nz
        other = j // (2 * near + 1)
        z = two_ways(j - other * (2 * near + 1))
        return at(sign * ((k // nz + j) % nx), sign * z, other)

    def plane_at(x, y, c):
        return {
            "slab": (my_x + nx + x) % nx * nz + my_z,
            "group": (my_y + ny + y) % ny * CORES + (core + c) % CORES,
        }

    def owner(k, sign):
        m = k % (nx * ny)
        return plane_at(sign * (m % nx), sign * ((m // nx + m % nx) % ny), k // (nx * ny))

    def z_peer(d):
        return {"slab": my_x * nz + (my_z + nz + d) % nz}

    def y_peer(dy):
        return {"group": (my_y + ny + dy) % ny * CORES + core}

    barrier = pltpu.get_barrier_semaphore()

    def each(first, last, action):
        def body(k, carry):
            action(k)
            return carry

        lax.fori_loop(first, last, body, 0)

    def greet(device):
        pl.semaphore_signal(barrier, inc=1, device_id=device, device_id_type=MESH)

    each(1, slabs, lambda k: greet(server(k, 1)))
    for dy in range(1, ny):
        each(0, nx * CORES, lambda i: greet(plane_at(i // CORES, dy, i % CORES)))
    greet(at(0, nz // 2, 0))
    greeted = slabs - 1 + (ny - 1) * nx * CORES + 1

    def half_copy(p):
        return pltpu.make_async_remote_copy(
            src_ref=vol_ref.at[my_y * PARTS + p], dst_ref=held.at[my_y * PARTS + p],
            send_sem=half_ss.at[p], recv_sem=half_rs.at[p], device_id=at(0, nz // 2, 0), device_id_type=MESH,
        )

    def share_copy(dy, p):
        i = dy * PARTS + p
        return pltpu.make_async_remote_copy(
            src_ref=held.at[my_y * PARTS + p], dst_ref=held.at[my_y * PARTS + p],
            send_sem=share_ss.at[i], recv_sem=share_rs.at[i], device_id=y_peer(dy), device_id_type=MESH,
        )

    @pl.when(core == 0)
    def _():
        held[...] = vol_ref[...]

    pl.semaphore_wait(barrier, greeted)

    @pl.when(core == 1)
    def _():
        each(0, PARTS, lambda p: half_copy(p).start())

    req = req_ref[...]
    req = jnp.concatenate([req[0:1], req[1:2]], axis=1)
    bucket, piece = req >> 10, req & 1023
    tile, slab_of = bucket % tiles, bucket // tiles
    dx = (slab_of // nz + nx - my_x) % nx
    dz = (slab_of % nz + nz - my_z) % nz
    away = (dz + nz - core * (nz // 2)) % nz
    other = ((away > near) & (away < nz - near)).astype(jnp.int32)
    away = jnp.where(other == 1, away - nz // 2, away - jnp.where(away > near, nz, 0))
    from_j = other * (2 * near + 1) + jnp.where(away > 0, 2 * away - 1, -2 * away)
    home = slab_of % nz
    dy = (home % ny + ny - my_y) % ny
    dc = (home // ny + CORES - core) % CORES
    from_k = (dx + nx * nz - from_j) % nx * nz + from_j
    to_k = (dc * ny + (dy + nx * ny - dx) % ny) * nx + dx
    both = 2 * items
    own = iota((slabs * tiles, both), 0) == slab_of * tiles + tile
    before = (iota((both, both), 0) < iota((both, both), 1)).astype(F32).astype(BF)
    earlier = mm(own.astype(F32).astype(BF), before)
    rank = jnp.sum(jnp.where(own, earlier, 0.0), axis=0, keepdims=True).astype(jnp.int32)
    seat = tile * cap + rank
    def pass_on_quarter(p):
        @pl.when(core == 1)
        def _():
            half_copy(p).wait_recv()
            for dy in range(1, ny):
                share_copy(dy, p).start()

    each(0, PARTS // 2, pass_on_quarter)
    from_spot, to_spot = from_k * chunk + seat, to_k * chunk + seat
    at_seat = iota((128, both), 0) == seat
    low = jnp.where(at_seat, (piece & 31).astype(F32), 0.0).astype(BF)
    high = jnp.where(at_seat, (piece >> 5).astype(F32), 0.0).astype(BF)
    def request_codes(step_k, out, own_in):
        chosen = (iota((slabs, both), 0) == step_k).astype(F32).astype(BF)
        codes = lax.dot_general(chosen, low, NT, preferred_element_type=F32)
        codes = codes + 32.0 * lax.dot_general(chosen, high, NT, preferred_element_type=F32)
        codes = codes.astype(jnp.int32)
        for k in range(slabs):
            out[k] = codes[k : k + 1]
        own_in[0] = codes[0:1]

    request_codes(from_k, code_out, code_in)

    def sum_copy(k):
        return pltpu.make_async_remote_copy(
            src_ref=sum_out.at[k], dst_ref=sum_in.at[k], send_sem=sum_ss.at[k], recv_sem=sum_rs.at[k],
            device_id=owner(k, 1), device_id_type=MESH,
        )

    def code_copy(k):
        return pltpu.make_async_remote_copy(
            src_ref=code_out.at[k], dst_ref=code_in.at[k], send_sem=code_ss.at[k], recv_sem=code_rs.at[k],
            device_id=server(k, 1), device_id_type=MESH,
        )

    def answer_copy(k):
        return pltpu.make_async_remote_copy(
            src_ref=send1.at[k], dst_ref=recv1.at[k], send_sem=ss1.at[k], recv_sem=rs1.at[k],
            device_id=server(k, -1), device_id_type=MESH,
        )

    def return_copy(k):
        return pltpu.make_async_remote_copy(
            src_ref=send2.at[k], dst_ref=recv2.at[k], send_sem=ss2.at[k], recv_sem=rs2.at[k],
            device_id=owner(k, 1), device_id_type=MESH,
        )

    each(1, slabs, lambda k: code_copy(k).start())

    each(PARTS // 2, PARTS, pass_on_quarter)

    @pl.when(core == 1)
    def _():
        for dy in range(1, ny):
            each(0, PARTS, lambda p: share_copy(dy, p).wait_recv())

    row_tile = iota((rows, box), 0) % chunk // cap

    def serve(b, carry):
        for c in range(per):
            k = b * per + c

            @pl.when(k > 0)
            def _():
                code_copy(k).wait_recv()

        for c in range(per):
            code = code_in[b * per + c].astype(F32)
            eye = iota((chunk, 128), 0) == iota((chunk, 128), 1)
            col = jnp.sum(jnp.where(eye, code, 0.0), axis=1, keepdims=True)
            hot[c * chunk : (c + 1) * chunk] = (iota((chunk, pieces), 1) == col.astype(jnp.int32)).astype(F32).astype(BF)
        fetched = mm(hot[...], held[...].reshape(pieces, width))
        for part in range(2):
            half = fetched[:, part * box : (part + 1) * box]
            answer = jnp.zeros((rows, box), F32)
            for t in range(tiles):
                answer = answer + mm(jnp.where(row_tile == t, half, 0.0).astype(BF), w_ref[t])
            send1[pl.ds(b * per, per), :, part * box : (part + 1) * box] = answer.astype(BF).reshape(per, chunk, box)
        for c in range(per):
            k = b * per + c

            @pl.when(k > 0)
            def _():
                answer_copy(k).start()

        return carry

    lax.fori_loop(0, BATCHES, serve, 0)
    recv1[0] = send1[0]

    request_codes(to_k, sum_out, sum_in)
    each(1, slabs, lambda k: sum_copy(k).start())

    spot0, spot1 = from_spot[:, :items], from_spot[:, items:]
    back0, back1 = to_spot[:, :items], to_spot[:, items:]
    diagonal = iota((items, items), 0) == iota((items, items), 1)
    col0 = jnp.sum(jnp.where(diagonal, spot0.astype(F32), 0.0), axis=1, keepdims=True).astype(jnp.int32)
    col1 = jnp.sum(jnp.where(diagonal, spot1.astype(F32), 0.0), axis=1, keepdims=True).astype(jnp.int32)
    for b in range(BATCHES):
        across = iota((items, rows), 1) + b * rows
        pick[b] = ((across == col0) | (across == col1)).astype(F32).astype(BF)
        down = iota((rows, items), 0) + b * rows
        place[b] = ((down == back0) | (down == back1)).astype(F32).astype(BF)

    each(1, slabs, lambda k: sum_copy(k).wait_recv())

    def code_line(b, carry):
        line = jnp.zeros((1, rows), F32)
        for c in range(per):
            eye = iota((chunk, 128), 0) == iota((chunk, 128), 1)
            col = jnp.sum(jnp.where(eye, sum_in[b * per + c].astype(F32), 0.0), axis=1, keepdims=True)
            spread = iota((chunk, rows), 0) + c * chunk == iota((chunk, rows), 1)
            line = line + jnp.sum(jnp.where(spread, col, 0.0), axis=0, keepdims=True)
        code_rows[b] = line.astype(jnp.int32)
        return carry

    lax.fori_loop(0, BATCHES, code_line, 0)

    number = iota((images, box), 0)
    shift = jnp.zeros((images, box), F32)
    for i in range(images):
        shift = jnp.where(number == i, (pose_ref[i] - POSES // 2).astype(F32), shift)
    phases = 2.0 * jnp.pi * shift * iota((images, box), 1).astype(F32) / box
    cos_table, sin_table = jnp.cos(phases), jnp.sin(phases)

    proj[...] = jnp.zeros_like(proj)

    def collect(b, carry):
        for c in range(per):
            k = b * per + c

            @pl.when(k > 0)
            def _():
                answer_copy(k).wait_recv()

        proj[...] += mm(pick[b], recv1[pl.ds(b * per, per)].reshape(rows, width))
        return carry

    lax.fori_loop(0, BATCHES, collect, 0)

    for i in range(images):
        part = slice(i * lines, (i + 1) * lines)
        real, imag = proj[part, :box], proj[part, box:]
        cos, sin = cos_table[i : i + 1], sin_table[i : i + 1]
        ctf = ctf_ref[cls_ref[i]]
        res_real = obs_ref[part, :box].astype(F32) - ctf * (real * cos - imag * sin)
        res_imag = obs_ref[part, box:].astype(F32) - ctf * (real * sin + imag * cos)
        res_ref[part, :box] = res_real.astype(BF)
        res_ref[part, box:] = res_imag.astype(BF)
        real, imag = ctf * res_real, ctf * res_imag
        ret[part, :box] = (real * cos + imag * sin).astype(BF)
        ret[part, box:] = (imag * cos - real * sin).astype(BF)

    def give_back(b, carry):
        filled = mm(place[b], ret[...]).astype(BF)
        send2[pl.ds(b * per, per)] = filled.reshape(per, chunk, width)
        for c in range(per):
            k = b * per + c

            @pl.when(k > 0)
            def _():
                return_copy(k).start()

        return carry

    lax.fori_loop(0, BATCHES, give_back, 0)
    recv2[0] = send2[0]
    total[...] = jnp.zeros_like(total)

    def add_parts(b, g):
        at_piece = iota((rows_added, rows), 0) + g * rows_added == code_rows[b]
        more = mm(at_piece.astype(F32).astype(BF), rows_back[...])
        total[pl.ds(g * TOGETHER, TOGETHER)] += more.reshape(TOGETHER, sum_rows, width)

    def absorb(b, carry):
        for c in range(per):
            k = b * per + c

            @pl.when(k > 0)
            def _():
                return_copy(k).wait_recv()

        got = recv2[pl.ds(b * per, per)].reshape(rows, width).astype(F32)
        for part in range(2):
            half = got[:, part * box : (part + 1) * box]
            back = jnp.zeros((rows, box), F32)
            for t in range(tiles):
                masked = jnp.where(row_tile == t, half, 0.0).astype(BF)
                back = back + lax.dot_general(masked, w_ref[t], NT, preferred_element_type=F32)
            rows_back[:, part * box : (part + 1) * box] = back.astype(BF)

        @pl.when(b < BATCHES - 1)
        def _():
            each(0, STEPS // TOGETHER, lambda g: add_parts(b, g))

        return carry

    lax.fori_loop(0, BATCHES, absorb, 0)

    root_y, root_core = my_z % ny, my_z // ny
    turn = (my_y + ny - root_y) % ny
    on_core = core == root_core
    last = BATCHES - 1
    half = nz // 2
    hops = (my_z + nz - my_y - ny * core) % nz
    way = 1 - 2 * (hops // (half + 1))
    tip = (hops == half) | (hops == half + 1)

    def chain_copy(p):
        return pltpu.make_async_remote_copy(
            src_ref=chain_out.at[p], dst_ref=chain_in.at[p], send_sem=chain_ss.at[p], recv_sem=chain_rs.at[p],
            device_id=z_peer(-way), device_id_type=MESH,
        )

    def root_copy(p):
        return pltpu.make_async_remote_copy(
            src_ref=chain_out.at[p], dst_ref=root_in.at[p], send_sem=chain_ss.at[p], recv_sem=root_rs.at[p],
            device_id=z_peer(1), device_id_type=MESH,
        )

    def y_copy(p, d, sem):
        return pltpu.make_async_remote_copy(
            src_ref=result.at[p], dst_ref=result.at[p], send_sem=sem.at[p], recv_sem=y_rs.at[p],
            device_id=y_peer(d), device_id_type=MESH,
        )

    def sibling_copy(p):
        return pltpu.make_async_remote_copy(
            src_ref=result.at[p], dst_ref=result.at[p], send_sem=sib_ss.at[p], recv_sem=sib_rs.at[p],
            device_id=sibling, device_id_type=MESH,
        )

    def goes_up(p):
        return on_core & ((turn == 0) | ((turn == 1) & (p % 2 == 0))) if ny > 2 else on_core & (turn == 0)

    def goes_down(p):
        return on_core & ((turn == 0) | ((turn == ny - 1) & (p % 2 == 1)))

    def pass_on(p):
        @pl.when(goes_up(p))
        def _():
            y_copy(p, 1, up_ss).start()

        if ny > 2:
            @pl.when(goes_down(p))
            def _():
                y_copy(p, -1, down_ss).start()

        @pl.when(on_core)
        def _():
            sibling_copy(p).start()

        back_ref[p] = result[p]

    def gather_sum(p):
        @pl.when(p % TOGETHER == 0)
        def _():
            add_parts(last, p // TOGETHER)

        @pl.when(jnp.logical_not(tip))
        def _():
            chain_copy(p).wait_recv()
            total[p] += chain_in[p].astype(F32)

        @pl.when(hops == 0)
        def _():
            root_copy(p).wait_recv()
            result[p] = (total[p] + root_in[p].astype(F32)).astype(BF)
            pass_on(p)

        @pl.when(hops > 0)
        def _():
            chain_out[p] = total[p].astype(BF)

        @pl.when((hops > 0) & (hops < nz - 1))
        def _():
            chain_copy(p).start()

        @pl.when(hops == nz - 1)
        def _():
            root_copy(p).start()

    def take_result(p):
        @pl.when(on_core & (turn > 0))
        def _():
            y_copy(p, 1, up_ss).wait_recv()
            pass_on(p)

        @pl.when(jnp.logical_not(on_core))
        def _():
            sibling_copy(p).wait_recv()
            pass_on(p)

    def sum_step(i):
        @pl.when(i < STEPS)
        def _():
            gather_sum(i)

        @pl.when(i >= STEPS)
        def _():
            take_result(i - STEPS)

    each(0, STEPS + STEPS, sum_step)

    def drain(k):
        code_copy(k).wait_send()
        sum_copy(k).wait_send()
        answer_copy(k).wait_send()
        return_copy(k).wait_send()

    def drain_step(p):
        @pl.when(hops > 0)
        def _():
            chain_copy(p).wait_send()

        @pl.when(goes_up(p))
        def _():
            y_copy(p, 1, up_ss).wait_send()

        if ny > 2:
            @pl.when(goes_down(p))
            def _():
                y_copy(p, -1, down_ss).wait_send()

        @pl.when(on_core)
        def _():
            sibling_copy(p).wait_send()

    each(1, slabs, drain)

    @pl.when(core == 1)
    def _():
        each(0, PARTS, lambda p: half_copy(p).wait_send())
        for dy in range(1, ny):
            each(0, PARTS, lambda p: share_copy(dy, p).wait_send())

    each(0, STEPS, drain_step)


def on_device(nx, nz, ny, volume, weight_tiles, ctf_table, observed, routes, piece_index, pose_index, ctf_class):
    pieces, _, box = volume.shape
    images, lines = observed.shape[:2]
    items = images * lines
    tiles = weight_tiles.shape[0]
    slabs = nx * nz
    cap = max(2, 4 * items // (slabs * tiles))
    per = slabs // BATCHES
    chunk = tiles * cap
    rows = per * chunk
    width = 2 * box
    sums = (STEPS, pieces // STEPS, width)
    parts = (ny * PARTS, pieces // (ny * PARTS), width)
    requests = (routes * 1024 + piece_index).transpose(2, 0, 1).reshape(2, items)
    vmem, smem = pl.BlockSpec(memory_space=pltpu.VMEM), pl.BlockSpec(memory_space=pltpu.SMEM)
    dma = pltpu.SemaphoreType.DMA
    back, residual = pl.pallas_call(
        functools.partial(kernel, (nx, nz, ny, tiles, cap, lines)),
        out_shape=(jax.ShapeDtypeStruct(sums, BF), jax.ShapeDtypeStruct((items, width), BF)),
        in_specs=[smem, smem, vmem, vmem, vmem, vmem, vmem],
        out_specs=(vmem, vmem),
        scratch_shapes=[
            pltpu.VMEM(parts, BF),
            *[pltpu.VMEM((slabs, 1, 128), jnp.int32)] * 4,
            pltpu.VMEM((BATCHES, 1, rows), jnp.int32),
            pltpu.VMEM((rows, pieces), BF),
            pltpu.VMEM((slabs, chunk, width), BF),
            pltpu.VMEM((slabs, chunk, width), BF),
            pltpu.VMEM((BATCHES, items, rows), BF),
            pltpu.VMEM((BATCHES, rows, items), BF),
            pltpu.VMEM((items, width), F32),
            pltpu.VMEM((items, width), BF),
            pltpu.VMEM((slabs, chunk, width), BF),
            pltpu.VMEM((slabs, chunk, width), BF),
            pltpu.VMEM((rows, width), BF),
            pltpu.VMEM(sums, F32),
            *[pltpu.VMEM(sums, BF)] * 4,
            *[dma((PARTS,))] * 2,
            *[dma((ny * PARTS,))] * 2,
            *[dma((slabs,))] * 8,
            *[dma((STEPS,))] * 8,
        ],
        compiler_params=pltpu.CompilerParams(collective_id=0, has_side_effects=True, vmem_limit_bytes=56 * 2**20),
    )(
        pose_index, ctf_class, requests, volume.reshape(parts), weight_tiles, ctf_table,
        observed.reshape(items, width),
    )
    return back.reshape(pieces, 2, box).astype(F32), residual.reshape(images, lines, 2, box)


def solution(mesh):
    slabs, groups = mesh.shape["slab"], mesh.shape["group"]
    nz = groups
    by_device = ("group", "slab")
    return jax.shard_map(
        functools.partial(on_device, slabs // nz, nz, groups // CORES),
        mesh=mesh,
        in_specs=(
            P("slab", None, None), P(), P(), P(by_device, None, None, None), P(by_device, None, None),
            P(by_device, None, None), P(by_device), P(by_device),
        ),
        out_specs=(P("slab", None, None), P(by_device, None, None, None)),
        check_vma=False,
    )
```

```python
import functools

import jax
import jax.numpy as jnp
from jax import lax
from jax.experimental import pallas as pl
from jax.experimental.pallas import tpu as pltpu
from jax.sharding import PartitionSpec as P

MESH = pl.DeviceIdType.MESH
POSES = 32
CORES = 2
BATCHES = 4
PARTS = 4
STEPS = 8
TOGETHER = 2
BF = jnp.bfloat16
F32 = jnp.float32
NT = (((1,), (1,)), ((), ()))


def mm(a, b):
    return jnp.dot(a, b, preferred_element_type=F32)


def iota(shape, axis):
    return lax.broadcasted_iota(jnp.int32, shape, axis)


def kernel(
    cfg,
    pose_ref, cls_ref, req_ref, vol_ref, w_ref, ctf_ref, obs_ref,
    back_ref, res_ref,
    seen, held, code_out, code_in, sum_out, sum_in, code_rows, hot, send1, recv1, pick, place, proj, ret, send2, recv2, rows_back, total,
    chain_out, chain_in, root_in, result,
    half_ss, half_rs, share_ss, share_rs, code_ss, code_rs, sum_ss, sum_rs, ss1, rs1, ss2, rs2, chain_ss, chain_rs, root_rs, up_ss, down_ss, y_rs, sib_ss, sib_rs,
):
    nx, nz, ny, tiles, cap, lines = cfg
    slabs = nx * nz
    per = slabs // BATCHES
    chunk = tiles * cap
    rows = per * chunk
    items = req_ref.shape[1]
    part_rows, width = vol_ref.shape[1:]
    pieces = ny * PARTS * part_rows
    box = width // 2
    sum_rows = pieces // STEPS
    rows_added = TOGETHER * sum_rows
    images = items // lines

    slab, group = lax.axis_index("slab"), lax.axis_index("group")
    my_x, my_z = slab // nz, slab % nz
    my_y, core = group // CORES, group % CORES
    sibling = {"group": my_y * CORES + 1 - core}

    near = nz // 4

    def at(x, z, c):
        return {"slab": (my_x + nx + x) % nx * nz + (my_z + 2 * nz + z) % nz, "group": my_y * CORES + (core + c) % CORES}

    def two_ways(j):
        return j % 2 * ((j + 1) // 2) - (1 - j % 2) * (j // 2)

    def server(k, sign):
        j = k % nz
        other = j // (2 * near + 1)
        z = two_ways(j - other * (2 * near + 1))
        return at(sign * ((k // nz + j) % nx), sign * z, other)

    def plane_at(x, y, c):
        return {
            "slab": (my_x + nx + x) % nx * nz + my_z,
            "group": (my_y + ny + y) % ny * CORES + (core + c) % CORES,
        }

    def owner(k, sign):
        m = k % (nx * ny)
        return plane_at(sign * (m % nx), sign * ((m // nx + m % nx) % ny), k // (nx * ny))

    def z_peer(d):
        return {"slab": my_x * nz + (my_z + nz + d) % nz}

    def y_peer(dy):
        return {"group": (my_y + ny + dy) % ny * CORES + core}

    barrier = pltpu.get_barrier_semaphore()

    def each(first, last, action):
        def body(k, carry):
            action(k)
            return carry

        lax.fori_loop(first, last, body, 0)

    def greet(device):
        pl.semaphore_signal(barrier, inc=1, device_id=device, device_id_type=MESH)

    each(1, slabs, lambda k: greet(server(k, 1)))
    for dy in range(1, ny):
        each(0, nx * CORES, lambda i: greet(plane_at(i // CORES, dy, i % CORES)))
    greet(at(0, nz // 2, 0))
    greeted = slabs - 1 + (ny - 1) * nx * CORES + 1

    def half_copy(p):
        return pltpu.make_async_remote_copy(
            src_ref=vol_ref.at[my_y * PARTS + p], dst_ref=held.at[my_y * PARTS + p],
            send_sem=half_ss.at[p], recv_sem=half_rs.at[p], device_id=at(0, nz // 2, 0), device_id_type=MESH,
        )

    def share_copy(dy, p):
        i = dy * PARTS + p
        return pltpu.make_async_remote_copy(
            src_ref=held.at[my_y * PARTS + p], dst_ref=held.at[my_y * PARTS + p],
            send_sem=share_ss.at[i], recv_sem=share_rs.at[i], device_id=y_peer(dy), device_id_type=MESH,
        )

    @pl.when(core == 0)
    def _():
        held[...] = vol_ref[...]

    req = req_ref[...]
    req = jnp.concatenate([req[0:1], req[1:2]], axis=1)
    bucket, piece = req >> 10, req & 1023
    tile, slab_of = bucket & tiles - 1, bucket >> tiles.bit_length() - 1
    home = slab_of & nz - 1
    dx = (slab_of >> nz.bit_length() - 1) + nx - my_x & nx - 1
    away = home + 2 * nz - my_z - core * (nz // 2) & nz - 1
    other = ((away > near) & (away < nz - near)).astype(jnp.int32)
    away = jnp.where(other == 1, away - nz // 2, away - jnp.where(away > near, nz, 0))
    from_j = other * (2 * near + 1) + jnp.where(away > 0, 2 * away - 1, -2 * away)
    dy = (home & ny - 1) + ny - my_y & ny - 1
    dc = (home >> ny.bit_length() - 1) + CORES - core & CORES - 1
    from_k = (dx + nx * nz - from_j & nx - 1) * nz + from_j
    to_k = (dc * ny + (dy + nx * ny - dx & ny - 1)) * nx + dx
    both = 2 * items
    own = iota((slabs * tiles, both), 0) == slab_of * tiles + tile
    before = (iota((both, both), 0) < iota((both, both), 1)).astype(F32).astype(BF)
    earlier = mm(own.astype(F32).astype(BF), before)
    rank = jnp.sum(jnp.where(own, earlier, 0.0), axis=0, keepdims=True).astype(jnp.int32)
    seat = tile * cap + rank
    def pass_on_quarter(p):
        @pl.when(core == 1)
        def _():
            half_copy(p).wait_recv()
            for dy in range(1, ny):
                share_copy(dy, p).start()

    from_spot, to_spot = from_k * chunk + seat, to_k * chunk + seat
    at_seat = iota((128, both), 0) == seat
    low = jnp.where(at_seat, (piece & 31).astype(F32), 0.0).astype(BF)
    high = jnp.where(at_seat, (piece >> 5).astype(F32), 0.0).astype(BF)
    def request_codes(step_k, out, own_in):
        chosen = (iota((slabs, both), 0) == step_k).astype(F32).astype(BF)
        codes = lax.dot_general(chosen, low, NT, preferred_element_type=F32)
        codes = codes + 32.0 * lax.dot_general(chosen, high, NT, preferred_element_type=F32)
        codes = codes.astype(jnp.int32)
        for k in range(slabs):
            out[k] = codes[k : k + 1]
        own_in[0] = codes[0:1]

    request_codes(from_k, code_out, code_in)
    pl.semaphore_wait(barrier, greeted)


    def sum_copy(k):
        return pltpu.make_async_remote_copy(
            src_ref=sum_out.at[k], dst_ref=sum_in.at[k], send_sem=sum_ss.at[k], recv_sem=sum_rs.at[k],
            device_id=owner(k, 1), device_id_type=MESH,
        )

    def code_copy(k):
        return pltpu.make_async_remote_copy(
            src_ref=code_out.at[k], dst_ref=code_in.at[k], send_sem=code_ss.at[k], recv_sem=code_rs.at[k],
            device_id=server(k, 1), device_id_type=MESH,
        )

    def answer_copy(k):
        return pltpu.make_async_remote_copy(
            src_ref=send1.at[k], dst_ref=recv1.at[k], send_sem=ss1.at[k], recv_sem=rs1.at[k],
            device_id=server(k, -1), device_id_type=MESH,
        )

    def return_copy(k):
        return pltpu.make_async_remote_copy(
            src_ref=send2.at[k], dst_ref=recv2.at[k], send_sem=ss2.at[k], recv_sem=rs2.at[k],
            device_id=owner(k, 1), device_id_type=MESH,
        )

    each(1, slabs, lambda k: code_copy(k).start())

    @pl.when(core == 1)
    def _():
        each(0, PARTS, lambda p: half_copy(p).start())

    each(0, PARTS, pass_on_quarter)

    @pl.when(core == 1)
    def _():
        for dy in range(1, ny):
            each(0, PARTS, lambda p: share_copy(dy, p).wait_recv())

    row_tile = sum((iota((per, chunk, box), 1) >= t * cap).astype(jnp.int32) for t in range(1, tiles))
    row_tile = row_tile.reshape(rows, box)

    def serve(b, carry):
        for c in range(per):
            k = b * per + c

            @pl.when(k > 0)
            def _():
                code_copy(k).wait_recv()

        for c in range(per):
            code = code_in[b * per + c].astype(F32)
            eye = iota((chunk, 128), 0) == iota((chunk, 128), 1)
            col = jnp.sum(jnp.where(eye, code, 0.0), axis=1, keepdims=True)
            hot[c * chunk : (c + 1) * chunk] = (iota((chunk, pieces), 1) == col.astype(jnp.int32)).astype(F32).astype(BF)
        fetched = mm(hot[...], held[...].reshape(pieces, width))
        for part in range(2):
            half = fetched[:, part * box : (part + 1) * box]
            answer = jnp.zeros((rows, box), F32)
            for t in range(tiles):
                answer = answer + mm(jnp.where(row_tile == t, half, 0.0).astype(BF), w_ref[t])
            send1[pl.ds(b * per, per), :, part * box : (part + 1) * box] = answer.astype(BF).reshape(per, chunk, box)
        for c in range(per):
            k = b * per + c

            @pl.when(k > 0)
            def _():
                answer_copy(k).start()

        return carry

    lax.fori_loop(0, BATCHES, serve, 0)
    recv1[0] = send1[0]

    request_codes(to_k, sum_out, sum_in)
    each(1, slabs, lambda k: sum_copy(k).start())

    spot0, spot1 = from_spot[:, :items], from_spot[:, items:]
    back0, back1 = to_spot[:, :items], to_spot[:, items:]
    diagonal = iota((items, items), 0) == iota((items, items), 1)
    col0 = jnp.sum(jnp.where(diagonal, spot0.astype(F32), 0.0), axis=1, keepdims=True).astype(jnp.int32)
    col1 = jnp.sum(jnp.where(diagonal, spot1.astype(F32), 0.0), axis=1, keepdims=True).astype(jnp.int32)
    for b in range(BATCHES):
        across = iota((items, rows), 1) + b * rows
        pick[b] = ((across == col0) | (across == col1)).astype(F32).astype(BF)
        down = iota((rows, items), 0) + b * rows
        place[b] = ((down == back0) | (down == back1)).astype(F32).astype(BF)

    each(1, slabs, lambda k: sum_copy(k).wait_recv())

    def code_line(b, carry):
        line = jnp.zeros((1, rows), F32)
        for c in range(per):
            eye = iota((chunk, 128), 0) == iota((chunk, 128), 1)
            col = jnp.sum(jnp.where(eye, sum_in[b * per + c].astype(F32), 0.0), axis=1, keepdims=True)
            spread = iota((chunk, rows), 0) + c * chunk == iota((chunk, rows), 1)
            line = line + jnp.sum(jnp.where(spread, col, 0.0), axis=0, keepdims=True)
        code_rows[b] = line.astype(jnp.int32)
        return carry

    lax.fori_loop(0, BATCHES, code_line, 0)

    number = iota((images, box), 0)
    shift = jnp.zeros((images, box), F32)
    for i in range(images):
        shift = jnp.where(number == i, (pose_ref[i] - POSES // 2).astype(F32), shift)
    phases = 2.0 * jnp.pi * shift * iota((images, box), 1).astype(F32) / box
    cos_table, sin_table = jnp.cos(phases), jnp.sin(phases)

    proj[...] = jnp.zeros_like(proj)
    for i in range(images):
        part = slice(i * lines, (i + 1) * lines)
        both_parts = obs_ref[part].astype(F32)
        seen[part, :box], seen[part, box:] = both_parts[:, 0].astype(BF), both_parts[:, 1].astype(BF)

    def collect(b, carry):
        for c in range(per):
            k = b * per + c

            @pl.when(k > 0)
            def _():
                answer_copy(k).wait_recv()

        proj[...] += mm(pick[b], recv1[pl.ds(b * per, per)].reshape(rows, width))
        return carry

    lax.fori_loop(0, BATCHES, collect, 0)

    for i in range(images):
        part = slice(i * lines, (i + 1) * lines)
        real, imag = proj[part, :box], proj[part, box:]
        cos, sin = cos_table[i : i + 1], sin_table[i : i + 1]
        ctf = ctf_ref[cls_ref[i]]
        res_real = seen[part, :box].astype(F32) - ctf * (real * cos - imag * sin)
        res_imag = seen[part, box:].astype(F32) - ctf * (real * sin + imag * cos)
        seen[part, :box], seen[part, box:] = res_real.astype(BF), res_imag.astype(BF)
        real, imag = ctf * res_real, ctf * res_imag
        ret[part, :box] = (real * cos + imag * sin).astype(BF)
        ret[part, box:] = (imag * cos - real * sin).astype(BF)

    def give_back(b, carry):
        filled = mm(place[b], ret[...]).astype(BF)
        send2[pl.ds(b * per, per)] = filled.reshape(per, chunk, width)
        for c in range(per):
            k = b * per + c

            @pl.when(k > 0)
            def _():
                return_copy(k).start()

        return carry

    lax.fori_loop(0, BATCHES, give_back, 0)
    recv2[0] = send2[0]
    total[...] = jnp.zeros_like(total)
    for i in range(images):
        part = slice(i * lines, (i + 1) * lines)
        both_parts = jnp.stack([seen[part, :box].astype(F32), seen[part, box:].astype(F32)], axis=1)
        res_ref[part] = both_parts.astype(BF)

    def add_parts(b, g):
        at_piece = iota((rows_added, rows), 0) + g * rows_added == code_rows[b]
        more = mm(at_piece.astype(F32).astype(BF), rows_back[...])
        total[pl.ds(g * TOGETHER, TOGETHER)] += more.reshape(TOGETHER, sum_rows, width)

    def absorb(b, carry):
        for c in range(per):
            k = b * per + c

            @pl.when(k > 0)
            def _():
                return_copy(k).wait_recv()

        got = recv2[pl.ds(b * per, per)].reshape(rows, width).astype(F32)
        for part in range(2):
            half = got[:, part * box : (part + 1) * box]
            back = jnp.zeros((rows, box), F32)
            for t in range(tiles):
                masked = jnp.where(row_tile == t, half, 0.0).astype(BF)
                back = back + lax.dot_general(masked, w_ref[t], NT, preferred_element_type=F32)
            rows_back[:, part * box : (part + 1) * box] = back.astype(BF)

        @pl.when(b < BATCHES - 1)
        def _():
            each(0, STEPS // TOGETHER, lambda g: add_parts(b, g))

        return carry

    lax.fori_loop(0, BATCHES, absorb, 0)

    root_y, root_core = my_z % ny, my_z // ny
    turn = (my_y + ny - root_y) % ny
    on_core = core == root_core
    last = BATCHES - 1
    half = nz // 2
    hops = (my_z + nz - my_y - ny * core) % nz
    way = 1 - 2 * (hops // (half + 1))
    tip = (hops == half) | (hops == half + 1)

    def chain_copy(p):
        return pltpu.make_async_remote_copy(
            src_ref=chain_out.at[p], dst_ref=chain_in.at[p], send_sem=chain_ss.at[p], recv_sem=chain_rs.at[p],
            device_id=z_peer(-way), device_id_type=MESH,
        )

    def root_copy(p):
        return pltpu.make_async_remote_copy(
            src_ref=chain_out.at[p], dst_ref=root_in.at[p], send_sem=chain_ss.at[p], recv_sem=root_rs.at[p],
            device_id=z_peer(1), device_id_type=MESH,
        )

    def y_copy(p, d, sem):
        return pltpu.make_async_remote_copy(
            src_ref=result.at[p], dst_ref=result.at[p], send_sem=sem.at[p], recv_sem=y_rs.at[p],
            device_id=y_peer(d), device_id_type=MESH,
        )

    def sibling_copy(p):
        return pltpu.make_async_remote_copy(
            src_ref=result.at[p], dst_ref=result.at[p], send_sem=sib_ss.at[p], recv_sem=sib_rs.at[p],
            device_id=sibling, device_id_type=MESH,
        )

    def goes_up(p):
        return on_core & ((turn == 0) | ((turn == 1) & (p % 2 == 0))) if ny > 2 else on_core & (turn == 0)

    def goes_down(p):
        return on_core & ((turn == 0) | ((turn == ny - 1) & (p % 2 == 1)))

    def pass_on(p):
        @pl.when(goes_up(p))
        def _():
            y_copy(p, 1, up_ss).start()

        if ny > 2:
            @pl.when(goes_down(p))
            def _():
                y_copy(p, -1, down_ss).start()

        @pl.when(on_core)
        def _():
            sibling_copy(p).start()

        back_ref[p] = result[p]

    def gather_sum(p):
        @pl.when(p % TOGETHER == 0)
        def _():
            add_parts(last, p // TOGETHER)

        @pl.when(jnp.logical_not(tip))
        def _():
            chain_copy(p).wait_recv()
            total[p] += chain_in[p].astype(F32)

        @pl.when(hops == 0)
        def _():
            root_copy(p).wait_recv()
            result[p] = (total[p] + root_in[p].astype(F32)).astype(BF)
            pass_on(p)

        @pl.when(hops > 0)
        def _():
            chain_out[p] = total[p].astype(BF)

        @pl.when((hops > 0) & (hops < nz - 1))
        def _():
            chain_copy(p).start()

        @pl.when(hops == nz - 1)
        def _():
            root_copy(p).start()

    def take_result(p):
        @pl.when(on_core & (turn > 0))
        def _():
            y_copy(p, 1, up_ss).wait_recv()
            pass_on(p)

        @pl.when(jnp.logical_not(on_core))
        def _():
            sibling_copy(p).wait_recv()
            pass_on(p)

    def sum_step(i):
        @pl.when(i < STEPS)
        def _():
            gather_sum(i)

        @pl.when(i >= STEPS)
        def _():
            take_result(i - STEPS)

    each(0, STEPS + STEPS, sum_step)

    def drain(k):
        code_copy(k).wait_send()
        sum_copy(k).wait_send()
        answer_copy(k).wait_send()
        return_copy(k).wait_send()

    def drain_step(p):
        @pl.when(hops > 0)
        def _():
            chain_copy(p).wait_send()

        @pl.when(goes_up(p))
        def _():
            y_copy(p, 1, up_ss).wait_send()

        if ny > 2:
            @pl.when(goes_down(p))
            def _():
                y_copy(p, -1, down_ss).wait_send()

        @pl.when(on_core)
        def _():
            sibling_copy(p).wait_send()

    each(1, slabs, drain)

    @pl.when(core == 1)
    def _():
        each(0, PARTS, lambda p: half_copy(p).wait_send())
        for dy in range(1, ny):
            each(0, PARTS, lambda p: share_copy(dy, p).wait_send())

    each(0, STEPS, drain_step)


def on_device(nx, nz, ny, volume, weight_tiles, ctf_table, observed, routes, piece_index, pose_index, ctf_class):
    pieces, _, box = volume.shape
    images, lines = observed.shape[:2]
    items = images * lines
    tiles = weight_tiles.shape[0]
    slabs = nx * nz
    cap = max(2, 4 * items // (slabs * tiles))
    per = slabs // BATCHES
    chunk = tiles * cap
    rows = per * chunk
    width = 2 * box
    sums = (STEPS, pieces // STEPS, width)
    parts = (ny * PARTS, pieces // (ny * PARTS), width)
    requests = (routes * 1024 + piece_index).transpose(2, 0, 1).reshape(2, items)
    vmem, smem = pl.BlockSpec(memory_space=pltpu.VMEM), pl.BlockSpec(memory_space=pltpu.SMEM)
    dma = pltpu.SemaphoreType.DMA
    back, residual = pl.pallas_call(
        functools.partial(kernel, (nx, nz, ny, tiles, cap, lines)),
        out_shape=(jax.ShapeDtypeStruct(sums, BF), jax.ShapeDtypeStruct((items, 2, box), BF)),
        in_specs=[smem, smem, vmem, vmem, vmem, vmem, vmem],
        out_specs=(vmem, vmem),
        scratch_shapes=[
            pltpu.VMEM((items, width), BF),
            pltpu.VMEM(parts, BF),
            *[pltpu.VMEM((slabs, 1, 128), jnp.int32)] * 4,
            pltpu.VMEM((BATCHES, 1, rows), jnp.int32),
            pltpu.VMEM((rows, pieces), BF),
            pltpu.VMEM((slabs, chunk, width), BF),
            pltpu.VMEM((slabs, chunk, width), BF),
            pltpu.VMEM((BATCHES, items, rows), BF),
            pltpu.VMEM((BATCHES, rows, items), BF),
            pltpu.VMEM((items, width), F32),
            pltpu.VMEM((items, width), BF),
            pltpu.VMEM((slabs, chunk, width), BF),
            pltpu.VMEM((slabs, chunk, width), BF),
            pltpu.VMEM((rows, width), BF),
            pltpu.VMEM(sums, F32),
            *[pltpu.VMEM(sums, BF)] * 4,
            *[dma((PARTS,))] * 2,
            *[dma((ny * PARTS,))] * 2,
            *[dma((slabs,))] * 8,
            *[dma((STEPS,))] * 8,
        ],
        compiler_params=pltpu.CompilerParams(collective_id=0, has_side_effects=True, vmem_limit_bytes=56 * 2**20),
    )(
        pose_index, ctf_class, requests, volume.reshape(parts), weight_tiles, ctf_table,
        observed.reshape(items, 2, box),
    )
    return back.reshape(pieces, 2, box).astype(F32), residual.reshape(images, lines, 2, box)


def solution(mesh):
    slabs, groups = mesh.shape["slab"], mesh.shape["group"]
    nz = groups
    by_device = ("group", "slab")
    return jax.shard_map(
        functools.partial(on_device, slabs // nz, nz, groups // CORES),
        mesh=mesh,
        in_specs=(
            P("slab", None, None), P(), P(), P(by_device, None, None, None), P(by_device, None, None),
            P(by_device, None, None), P(by_device), P(by_device),
        ),
        out_specs=(P("slab", None, None), P(by_device, None, None, None)),
        check_vma=False,
    )
```

```python
import functools

import jax
import jax.numpy as jnp
from jax import lax
from jax.experimental import pallas as pl
from jax.experimental.pallas import tpu as pltpu
from jax.sharding import PartitionSpec as P

MESH = pl.DeviceIdType.MESH
POSES = 32
CORES = 2
BATCHES = 4
PARTS = 4
STEPS = 8
TOGETHER = 2
LAG = 8
BF = jnp.bfloat16
F32 = jnp.float32
NT = (((1,), (1,)), ((), ()))


def mm(a, b):
    return jnp.dot(a, b, preferred_element_type=F32)


def iota(shape, axis):
    return lax.broadcasted_iota(jnp.int32, shape, axis)


def kernel(
    cfg,
    pose_ref, cls_ref, req_ref, vol_ref, w_ref, ctf_ref, obs_ref,
    back_ref, res_ref,
    seen, held, code_out, code_in, sum_out, sum_in, code_rows, hot, send1, recv1, pick, place, proj, ret, send2, recv2, rows_back, total,
    chain_out, chain_in, root_in, result,
    half_ss, half_rs, share_ss, share_rs, code_ss, code_rs, sum_ss, sum_rs, ss1, rs1, ss2, rs2, chain_ss, chain_rs, root_rs, up_ss, down_ss, y_rs, sib_ss, sib_rs,
):
    nx, nz, ny, tiles, cap, lines = cfg
    slabs = nx * nz
    per = slabs // BATCHES
    chunk = tiles * cap
    rows = per * chunk
    items = req_ref.shape[1]
    pieces, width = vol_ref.shape
    part_rows = pieces // (ny * PARTS)
    box = width // 2
    sum_rows = pieces // STEPS
    rows_added = TOGETHER * sum_rows
    images = items // lines

    slab, group = lax.axis_index("slab"), lax.axis_index("group")
    my_x, my_z = slab // nz, slab % nz
    my_y, core = group // CORES, group % CORES
    sibling = {"group": my_y * CORES + 1 - core}

    near = nz // 4

    def at(x, z, c):
        return {"slab": (my_x + nx + x) % nx * nz + (my_z + 2 * nz + z) % nz, "group": my_y * CORES + (core + c) % CORES}

    def two_ways(j):
        return j % 2 * ((j + 1) // 2) - (1 - j % 2) * (j // 2)

    def server(k, sign):
        j = k % nz
        other = j // (2 * near + 1)
        z = two_ways(j - other * (2 * near + 1))
        return at(sign * ((k // nz + j) % nx), sign * z, other)

    def plane_at(x, y, c):
        return {
            "slab": (my_x + nx + x) % nx * nz + my_z,
            "group": (my_y + ny + y) % ny * CORES + (core + c) % CORES,
        }

    def owner(k, sign):
        m = k % (nx * ny)
        return plane_at(sign * (m % nx), sign * ((m // nx + m % nx) % ny), k // (nx * ny))

    def z_peer(d):
        return {"slab": my_x * nz + (my_z + nz + d) % nz}

    def y_peer(dy):
        return {"group": (my_y + ny + dy) % ny * CORES + core}

    barrier = pltpu.get_barrier_semaphore()

    def each(first, last, action):
        def body(k, carry):
            action(k)
            return carry

        lax.fori_loop(first, last, body, 0)

    def greet(device):
        pl.semaphore_signal(barrier, inc=1, device_id=device, device_id_type=MESH)

    each(1, slabs, lambda k: greet(server(k, 1)))
    for dy in range(1, ny):
        each(0, nx * CORES, lambda i: greet(plane_at(i // CORES, dy, i % CORES)))
    greet(at(0, nz // 2, 0))
    greeted = slabs - 1 + (ny - 1) * nx * CORES + 1

    def half_copy(p):
        return pltpu.make_async_remote_copy(
            src_ref=vol_ref.at[pl.ds(pl.multiple_of((my_y * PARTS + p) * part_rows, part_rows), part_rows)],
            dst_ref=held.at[my_y * PARTS + p],
            send_sem=half_ss.at[p], recv_sem=half_rs.at[p], device_id=at(0, nz // 2, 0), device_id_type=MESH,
        )

    def share_copy(dy, p):
        i = dy * PARTS + p
        return pltpu.make_async_remote_copy(
            src_ref=held.at[my_y * PARTS + p], dst_ref=held.at[my_y * PARTS + p],
            send_sem=share_ss.at[i], recv_sem=share_rs.at[i], device_id=y_peer(dy), device_id_type=MESH,
        )

    @pl.when(core == 0)
    def _():
        held[...] = vol_ref[...].reshape(held.shape)

    req = req_ref[...]
    req = jnp.concatenate([req[0:1], req[1:2]], axis=1)
    bucket, piece = req >> 10, req & 1023
    tile, slab_of = bucket & tiles - 1, bucket >> tiles.bit_length() - 1
    home = slab_of & nz - 1
    dx = (slab_of >> nz.bit_length() - 1) + nx - my_x & nx - 1
    away = home + 2 * nz - my_z - core * (nz // 2) & nz - 1
    other = ((away > near) & (away < nz - near)).astype(jnp.int32)
    away = jnp.where(other == 1, away - nz // 2, away - jnp.where(away > near, nz, 0))
    from_j = other * (2 * near + 1) + jnp.where(away > 0, 2 * away - 1, -2 * away)
    dy = (home & ny - 1) + ny - my_y & ny - 1
    dc = (home >> ny.bit_length() - 1) + CORES - core & CORES - 1
    from_k = (dx + nx * nz - from_j & nx - 1) * nz + from_j
    to_k = (dc * ny + (dy + nx * ny - dx & ny - 1)) * nx + dx
    both = 2 * items
    own = iota((slabs * tiles, both), 0) == slab_of * tiles + tile
    before = (iota((both, both), 0) < iota((both, both), 1)).astype(F32).astype(BF)
    earlier = mm(own.astype(F32).astype(BF), before)
    rank = jnp.sum(jnp.where(own, earlier, 0.0), axis=0, keepdims=True).astype(jnp.int32)
    seat = tile * cap + rank
    def pass_on_quarter(p):
        @pl.when(core == 1)
        def _():
            half_copy(p).wait_recv()
            for dy in range(1, ny):
                share_copy(dy, p).start()

    from_spot, to_spot = from_k * chunk + seat, to_k * chunk + seat
    at_seat = iota((128, both), 0) == seat
    low = jnp.where(at_seat, (piece & 31).astype(F32), 0.0).astype(BF)
    high = jnp.where(at_seat, (piece >> 5).astype(F32), 0.0).astype(BF)
    def request_codes(step_k, out, own_in):
        chosen = (iota((slabs, both), 0) == step_k).astype(F32).astype(BF)
        codes = lax.dot_general(chosen, low, NT, preferred_element_type=F32)
        codes = codes + 32.0 * lax.dot_general(chosen, high, NT, preferred_element_type=F32)
        codes = codes.astype(jnp.int32)
        for k in range(slabs):
            out[k] = codes[k : k + 1]
        own_in[0] = codes[0:1]

    request_codes(from_k, code_out, code_in)
    pl.semaphore_wait(barrier, greeted)


    def sum_copy(k):
        return pltpu.make_async_remote_copy(
            src_ref=sum_out.at[k], dst_ref=sum_in.at[k], send_sem=sum_ss.at[k], recv_sem=sum_rs.at[k],
            device_id=owner(k, 1), device_id_type=MESH,
        )

    def code_copy(k):
        return pltpu.make_async_remote_copy(
            src_ref=code_out.at[k], dst_ref=code_in.at[k], send_sem=code_ss.at[k], recv_sem=code_rs.at[k],
            device_id=server(k, 1), device_id_type=MESH,
        )

    def answer_copy(k):
        return pltpu.make_async_remote_copy(
            src_ref=send1.at[k], dst_ref=recv1.at[k], send_sem=ss1.at[k], recv_sem=rs1.at[k],
            device_id=server(k, -1), device_id_type=MESH,
        )

    def return_copy(k):
        return pltpu.make_async_remote_copy(
            src_ref=send2.at[k], dst_ref=recv2.at[k], send_sem=ss2.at[k], recv_sem=rs2.at[k],
            device_id=owner(k, 1), device_id_type=MESH,
        )

    each(1, slabs, lambda k: code_copy(k).start())

    @pl.when(core == 1)
    def _():
        each(0, PARTS, lambda p: half_copy(p).start())

    each(0, PARTS, pass_on_quarter)

    @pl.when(core == 1)
    def _():
        for dy in range(1, ny):
            each(0, PARTS, lambda p: share_copy(dy, p).wait_recv())

    row_tile = sum((iota((per, chunk, box), 1) >= t * cap).astype(jnp.int32) for t in range(1, tiles))
    row_tile = row_tile.reshape(rows, box)

    def serve(b, carry):
        for c in range(per):
            k = b * per + c

            @pl.when(k > 0)
            def _():
                code_copy(k).wait_recv()

        for c in range(per):
            code = code_in[b * per + c].astype(F32)
            eye = iota((chunk, 128), 0) == iota((chunk, 128), 1)
            col = jnp.sum(jnp.where(eye, code, 0.0), axis=1, keepdims=True)
            hot[c * chunk : (c + 1) * chunk] = (iota((chunk, pieces), 1) == col.astype(jnp.int32)).astype(F32).astype(BF)
        fetched = mm(hot[...], held[...].reshape(pieces, width))
        for part in range(2):
            half = fetched[:, part * box : (part + 1) * box]
            answer = jnp.zeros((rows, box), F32)
            for t in range(tiles):
                answer = answer + mm(jnp.where(row_tile == t, half, 0.0).astype(BF), w_ref[t])
            send1[pl.ds(b * per, per), :, part * box : (part + 1) * box] = answer.astype(BF).reshape(per, chunk, box)
        for c in range(per):
            k = b * per + c

            @pl.when(k > 0)
            def _():
                answer_copy(k).start()

        return carry

    lax.fori_loop(0, BATCHES, serve, 0)
    recv1[0] = send1[0]

    request_codes(to_k, sum_out, sum_in)
    each(1, slabs, lambda k: sum_copy(k).start())

    spot0, spot1 = from_spot[:, :items], from_spot[:, items:]
    back0, back1 = to_spot[:, :items], to_spot[:, items:]
    diagonal = iota((items, items), 0) == iota((items, items), 1)
    col0 = jnp.sum(jnp.where(diagonal, spot0.astype(F32), 0.0), axis=1, keepdims=True).astype(jnp.int32)
    col1 = jnp.sum(jnp.where(diagonal, spot1.astype(F32), 0.0), axis=1, keepdims=True).astype(jnp.int32)
    for b in range(BATCHES):
        across = iota((items, rows), 1) + b * rows
        pick[b] = ((across == col0) | (across == col1)).astype(F32).astype(BF)
        down = iota((rows, items), 0) + b * rows
        place[b] = ((down == back0) | (down == back1)).astype(F32).astype(BF)

    each(1, slabs, lambda k: sum_copy(k).wait_recv())

    def code_line(b, carry):
        line = jnp.zeros((1, rows), F32)
        for c in range(per):
            eye = iota((chunk, 128), 0) == iota((chunk, 128), 1)
            col = jnp.sum(jnp.where(eye, sum_in[b * per + c].astype(F32), 0.0), axis=1, keepdims=True)
            spread = iota((chunk, rows), 0) + c * chunk == iota((chunk, rows), 1)
            line = line + jnp.sum(jnp.where(spread, col, 0.0), axis=0, keepdims=True)
        code_rows[b] = line.astype(jnp.int32)
        return carry

    lax.fori_loop(0, BATCHES, code_line, 0)

    number = iota((images, box), 0)
    shift = jnp.zeros((images, box), F32)
    for i in range(images):
        shift = jnp.where(number == i, (pose_ref[i] - POSES // 2).astype(F32), shift)
    phases = 2.0 * jnp.pi * shift * iota((images, box), 1).astype(F32) / box
    cos_table, sin_table = jnp.cos(phases), jnp.sin(phases)

    proj[...] = jnp.zeros_like(proj)
    for i in range(images):
        part = slice(i * lines, (i + 1) * lines)
        both_parts = obs_ref[part].astype(F32)
        seen[part, :box], seen[part, box:] = both_parts[:, 0].astype(BF), both_parts[:, 1].astype(BF)

    def collect(b, carry):
        for c in range(per):
            k = b * per + c

            @pl.when(k > 0)
            def _():
                answer_copy(k).wait_recv()

        proj[...] += mm(pick[b], recv1[pl.ds(b * per, per)].reshape(rows, width))
        return carry

    lax.fori_loop(0, BATCHES, collect, 0)

    for i in range(images):
        part = slice(i * lines, (i + 1) * lines)
        real, imag = proj[part, :box], proj[part, box:]
        cos, sin = cos_table[i : i + 1], sin_table[i : i + 1]
        ctf = ctf_ref[cls_ref[i]]
        res_real = seen[part, :box].astype(F32) - ctf * (real * cos - imag * sin)
        res_imag = seen[part, box:].astype(F32) - ctf * (real * sin + imag * cos)
        seen[part, :box], seen[part, box:] = res_real.astype(BF), res_imag.astype(BF)
        real, imag = ctf * res_real, ctf * res_imag
        ret[part, :box] = (real * cos + imag * sin).astype(BF)
        ret[part, box:] = (imag * cos - real * sin).astype(BF)

    def give_back(b, carry):
        filled = mm(place[b], ret[...]).astype(BF)
        send2[pl.ds(b * per, per)] = filled.reshape(per, chunk, width)
        for c in range(per):
            k = b * per + c

            @pl.when(k > 0)
            def _():
                return_copy(k).start()

        return carry

    lax.fori_loop(0, BATCHES, give_back, 0)
    recv2[0] = send2[0]
    total[...] = jnp.zeros_like(total)
    for i in range(images):
        part = slice(i * lines, (i + 1) * lines)
        both_parts = jnp.stack([seen[part, :box].astype(F32), seen[part, box:].astype(F32)], axis=1)
        res_ref[part] = both_parts.astype(BF)

    def add_parts(b, g):
        at_piece = iota((rows_added, rows), 0) + g * rows_added == code_rows[b]
        more = mm(at_piece.astype(F32).astype(BF), rows_back[...])
        total[pl.ds(g * TOGETHER, TOGETHER)] += more.reshape(TOGETHER, sum_rows, width)

    def absorb(b, carry):
        for c in range(per):
            k = b * per + c

            @pl.when(k > 0)
            def _():
                return_copy(k).wait_recv()

        got = recv2[pl.ds(b * per, per)].reshape(rows, width).astype(F32)
        for part in range(2):
            half = got[:, part * box : (part + 1) * box]
            back = jnp.zeros((rows, box), F32)
            for t in range(tiles):
                masked = jnp.where(row_tile == t, half, 0.0).astype(BF)
                back = back + lax.dot_general(masked, w_ref[t], NT, preferred_element_type=F32)
            rows_back[:, part * box : (part + 1) * box] = back.astype(BF)

        @pl.when(b < BATCHES - 1)
        def _():
            each(0, STEPS // TOGETHER, lambda g: add_parts(b, g))

        return carry

    lax.fori_loop(0, BATCHES, absorb, 0)

    root_y, root_core = my_z % ny, my_z // ny
    turn = (my_y + ny - root_y) % ny
    on_core = core == root_core
    last = BATCHES - 1
    half = nz // 2
    hops = (my_z + nz - my_y - ny * core) % nz
    way = 1 - 2 * (hops // (half + 1))
    tip = (hops == half) | (hops == half + 1)

    def chain_copy(p):
        return pltpu.make_async_remote_copy(
            src_ref=chain_out.at[p], dst_ref=chain_in.at[p], send_sem=chain_ss.at[p], recv_sem=chain_rs.at[p],
            device_id=z_peer(-way), device_id_type=MESH,
        )

    def root_copy(p):
        return pltpu.make_async_remote_copy(
            src_ref=chain_out.at[p], dst_ref=root_in.at[p], send_sem=chain_ss.at[p], recv_sem=root_rs.at[p],
            device_id=z_peer(1), device_id_type=MESH,
        )

    def y_copy(p, d, sem):
        return pltpu.make_async_remote_copy(
            src_ref=result.at[p], dst_ref=result.at[p], send_sem=sem.at[p], recv_sem=y_rs.at[p],
            device_id=y_peer(d), device_id_type=MESH,
        )

    def sibling_copy(p):
        return pltpu.make_async_remote_copy(
            src_ref=result.at[p], dst_ref=result.at[p], send_sem=sib_ss.at[p], recv_sem=sib_rs.at[p],
            device_id=sibling, device_id_type=MESH,
        )

    def goes_up(p):
        return on_core & ((turn == 0) | ((turn == 1) & (p % 2 == 0))) if ny > 2 else on_core & (turn == 0)

    def goes_down(p):
        return on_core & ((turn == 0) | ((turn == ny - 1) & (p % 2 == 1)))

    def pass_on(p):
        @pl.when(goes_up(p))
        def _():
            y_copy(p, 1, up_ss).start()

        if ny > 2:
            @pl.when(goes_down(p))
            def _():
                y_copy(p, -1, down_ss).start()

        @pl.when(on_core)
        def _():
            sibling_copy(p).start()

        done = result[p].astype(F32)
        done = jnp.stack([done[:, :box], done[:, box:]], axis=1)
        back_ref[pl.ds(p * sum_rows, sum_rows)] = done.astype(BF)

    def gather_sum(p):
        @pl.when(p % TOGETHER == 0)
        def _():
            add_parts(last, p // TOGETHER)

        @pl.when(jnp.logical_not(tip))
        def _():
            chain_copy(p).wait_recv()
            total[p] += chain_in[p].astype(F32)

        @pl.when(hops == 0)
        def _():
            root_copy(p).wait_recv()
            result[p] = (total[p] + root_in[p].astype(F32)).astype(BF)
            pass_on(p)

        @pl.when(hops > 0)
        def _():
            chain_out[p] = total[p].astype(BF)

        @pl.when((hops > 0) & (hops < nz - 1))
        def _():
            chain_copy(p).start()

        @pl.when(hops == nz - 1)
        def _():
            root_copy(p).start()

    def take_result(p):
        @pl.when(on_core & (turn > 0))
        def _():
            y_copy(p, 1, up_ss).wait_recv()
            pass_on(p)

        @pl.when(jnp.logical_not(on_core))
        def _():
            sibling_copy(p).wait_recv()
            pass_on(p)

    def sum_step(i):
        @pl.when(i < STEPS)
        def _():
            gather_sum(i)

        @pl.when(i >= LAG)
        def _():
            take_result(i - LAG)

    each(0, STEPS + LAG, sum_step)

    def drain(k):
        code_copy(k).wait_send()
        sum_copy(k).wait_send()
        answer_copy(k).wait_send()
        return_copy(k).wait_send()

    def drain_step(p):
        @pl.when(hops > 0)
        def _():
            chain_copy(p).wait_send()

        @pl.when(goes_up(p))
        def _():
            y_copy(p, 1, up_ss).wait_send()

        if ny > 2:
            @pl.when(goes_down(p))
            def _():
                y_copy(p, -1, down_ss).wait_send()

        @pl.when(on_core)
        def _():
            sibling_copy(p).wait_send()

    each(1, slabs, drain)

    @pl.when(core == 1)
    def _():
        each(0, PARTS, lambda p: half_copy(p).wait_send())
        for dy in range(1, ny):
            each(0, PARTS, lambda p: share_copy(dy, p).wait_send())

    each(0, STEPS, drain_step)


def on_device(nx, nz, ny, volume, weight_tiles, ctf_table, observed, routes, piece_index, pose_index, ctf_class):
    pieces, _, box = volume.shape
    images, lines = observed.shape[:2]
    items = images * lines
    tiles = weight_tiles.shape[0]
    slabs = nx * nz
    cap = max(2, 4 * items // (slabs * tiles))
    per = slabs // BATCHES
    chunk = tiles * cap
    rows = per * chunk
    width = 2 * box
    sums = (STEPS, pieces // STEPS, width)
    parts = (ny * PARTS, pieces // (ny * PARTS), width)
    requests = (routes * 1024 + piece_index).transpose(2, 0, 1).reshape(2, items)
    vmem, smem = pl.BlockSpec(memory_space=pltpu.VMEM), pl.BlockSpec(memory_space=pltpu.SMEM)
    dma = pltpu.SemaphoreType.DMA
    back, residual = pl.pallas_call(
        functools.partial(kernel, (nx, nz, ny, tiles, cap, lines)),
        out_shape=(jax.ShapeDtypeStruct((pieces, 2, box), BF), jax.ShapeDtypeStruct((items, 2, box), BF)),
        in_specs=[smem, smem, vmem, vmem, vmem, vmem, vmem],
        out_specs=(vmem, vmem),
        scratch_shapes=[
            pltpu.VMEM((items, width), BF),
            pltpu.VMEM(parts, BF),
            *[pltpu.VMEM((slabs, 1, 128), jnp.int32)] * 4,
            pltpu.VMEM((BATCHES, 1, rows), jnp.int32),
            pltpu.VMEM((rows, pieces), BF),
            pltpu.VMEM((slabs, chunk, width), BF),
            pltpu.VMEM((slabs, chunk, width), BF),
            pltpu.VMEM((BATCHES, items, rows), BF),
            pltpu.VMEM((BATCHES, rows, items), BF),
            pltpu.VMEM((items, width), F32),
            pltpu.VMEM((items, width), BF),
            pltpu.VMEM((slabs, chunk, width), BF),
            pltpu.VMEM((slabs, chunk, width), BF),
            pltpu.VMEM((rows, width), BF),
            pltpu.VMEM(sums, F32),
            *[pltpu.VMEM(sums, BF)] * 4,
            *[dma((PARTS,))] * 2,
            *[dma((ny * PARTS,))] * 2,
            *[dma((slabs,))] * 8,
            *[dma((STEPS,))] * 8,
        ],
        compiler_params=pltpu.CompilerParams(collective_id=0, has_side_effects=True, vmem_limit_bytes=56 * 2**20),
    )(
        pose_index, ctf_class, requests, volume.reshape(pieces, width), weight_tiles, ctf_table,
        observed.reshape(items, 2, box),
    )
    return back.astype(F32), residual.reshape(images, lines, 2, box)


def solution(mesh):
    slabs, groups = mesh.shape["slab"], mesh.shape["group"]
    nz = groups
    by_device = ("group", "slab")
    return jax.shard_map(
        functools.partial(on_device, slabs // nz, nz, groups // CORES),
        mesh=mesh,
        in_specs=(
            P("slab", None, None), P(), P(), P(by_device, None, None, None), P(by_device, None, None),
            P(by_device, None, None), P(by_device), P(by_device),
        ),
        out_specs=(P("slab", None, None), P(by_device, None, None, None)),
        check_vma=False,
    )
```
